1024 devices in a mesh: stn: 32 (over y_hi, x, core), chan: 8 (over z), tchunk: 4 (over y_lo).
Axes of the slice: x: 8, y: 8 (y_hi: 2, y_lo: 4; y = y_hi * 4 + y_lo), z: 8, core: 2. Of those that a mesh axis runs over, the one named last changes fastest.
Arguments:
- voltages: bfloat16 [512, 8, 512, 512], P('stn', 'chan', 'tchunk'), may hold values from -6 to 6
- weights: bfloat16 [512, 8, 2, 32, 256], P('stn', 'chan'), may hold values from -0.25 to 0.25
Outputs:
- visibilities: float32 [2, 8, 32, 512, 512], P(None, 'chan', 'stn', 'tchunk')
The draws below stay inside these ranges and needn't reach their ends.
All inputs are finite; a program needn't handle non-finite values.
Results may differ from the reference program's by a relative error of at most 0.0029.
Values may be sent and summed in bfloat16 or wider, within the bound.
No kernel may reach another device: no remote copies, remote signals or barrier semaphores. Data moves between devices by JAX's collectives and lax.ppermute only.
A program may use at most 32 MiB of HBM per device.

```python
import jax
import jax.numpy as jnp
from jax import lax

S = 512
E = 256
NB = 32
F = 8
NT = 512


def block_levels(rng, dims, cuts, low, largest):
    def one(axis_at, blocks):
        heights = jax.random.uniform(jax.random.fold_in(jax.random.fold_in(rng, 6), axis_at), (blocks,), jnp.float32, low / len(cuts), largest / len(cuts))
        return jnp.repeat(jnp.exp(heights), dims[axis_at] // blocks).reshape((-1,) + (1,) * (len(dims) - axis_at - 1))

    gain = one(*cuts[0])
    for cut in cuts[1:]:
        gain = gain * one(*cut)
    return gain


def centred(key, extent, spread, limit, pieces=(), kind=jnp.bfloat16):
    array = jax.random.normal(key, extent, jnp.float32) * spread
    if len(pieces) > 0:
        array = block_levels(key, extent, pieces, -0.22, 0.18) * array
    return jnp.clip(array, min=-limit, max=limit).astype(kind)


def setup_inputs(seed: int = 0) -> dict:
    splits = jax.random.split(jax.random.key(seed), 3)
    voltages = centred(splits[0], (S, F, NT, 2 * E), 1.0, 6.0, ((0, 32), (1, 8), (2, 4)))
    weights = centred(splits[1], (S, F, 2, NB, E), (2 * E) ** -0.5, 0.25, ((0, 32), (1, 8)))
    return dict(voltages=voltages, weights=weights)


def one_channel(volt, wgt):
    w_re = wgt[:, 0]
    w_im = wgt[:, 1]
    upper = jnp.concatenate([w_re, -w_im], axis=-1)
    lower = jnp.concatenate([w_im, w_re], axis=-1)
    matrix = jnp.concatenate([upper, lower], axis=1)
    beams = jnp.einsum('stk,sck->sct', volt.astype(jnp.float32), matrix.astype(jnp.float32))
    beams = beams.astype(jnp.bfloat16)
    real_part = beams[:, :NB, :]
    imag_part = beams[:, NB:, :]

    def per_beam(index):
        b_re = real_part[:, index, :]
        b_im = imag_part[:, index, :]
        left = jnp.concatenate([b_re, b_im], axis=-1)
        other = jnp.concatenate([b_im, -b_re], axis=-1)
        vis_re = jnp.dot(left, left.T, preferred_element_type=jnp.float32)
        vis_im = jnp.dot(other, left.T, preferred_element_type=jnp.float32)
        return jnp.stack([vis_re, vis_im]) / NT

    return lax.map(per_beam, jnp.arange(NB, dtype=jnp.int32))


def reference(voltages, weights):
    def per_channel(index):
        return one_channel(voltages[:, index], weights[:, index])

    result = lax.map(per_channel, jnp.arange(F, dtype=jnp.int32))
    return jnp.transpose(result, (2, 0, 1, 3, 4))
```

```python
import jax
import jax.numpy as jnp
from jax import lax
from jax.experimental import pallas as pl
from jax.experimental.pallas import tpu as pltpu
from jax.sharding import PartitionSpec as P

NT_DIMS = (((1,), (1,)), ((), ()))


def form_beams(copies, volt_ref, wgt_ref, out_ref, held):
    stations, beam_count = wgt_ref.shape[0], wgt_ref.shape[2]
    for s in range(stations):
        w_re = wgt_ref[s, 0]
        w_im = wgt_ref[s, 1]
        upper = jnp.concatenate([w_re, -w_im], axis=-1)
        lower = jnp.concatenate([w_im, w_re], axis=-1)
        matrix = jnp.concatenate([upper, lower], axis=0)
        formed = lax.dot_general(matrix, volt_ref[s], NT_DIMS, preferred_element_type=jnp.float32)
        held[:, 0, s, :] = formed[:beam_count]
        held[:, 1, s, :] = formed[beam_count:]
    rounded = held[...].astype(jnp.bfloat16)
    for c in range(copies):
        out_ref[:, c] = rounded


def correlate(scale, row_ref, beams_ref, out_ref):
    groups, times = beams_ref.shape[0], beams_ref.shape[1]
    stations, samples = beams_ref.shape[3], beams_ref.shape[4]
    row_groups = out_ref.shape[1] // stations
    first = row_ref[0] * row_groups
    vis_re = vis_im = None
    for t in range(times):
        re = beams_ref[:, t, 0].reshape(groups * stations, samples)
        im = beams_ref[:, t, 1].reshape(groups * stations, samples)
        left = jnp.concatenate([re, im], axis=-1)
        row_re = beams_ref[pl.ds(first, row_groups), t, 0].reshape(row_groups * stations, samples)
        row_im = beams_ref[pl.ds(first, row_groups), t, 1].reshape(row_groups * stations, samples)
        left_rows = jnp.concatenate([row_re, row_im], axis=-1)
        other_rows = jnp.concatenate([row_im, -row_re], axis=-1)
        rows = jnp.concatenate([left_rows, other_rows], axis=0)
        part = lax.dot_general(rows, left, NT_DIMS, preferred_element_type=jnp.float32)
        vis_re = part if vis_re is None else vis_re + part
    out_ref[...] = (vis_re * scale).reshape(out_ref.shape)


def local(voltages, weights):
    stations, _, samples, width = voltages.shape
    beam_count = weights.shape[3]
    times = lax.axis_size("tchunk")
    groups = lax.axis_size("stn")
    vmem = pl.BlockSpec(memory_space=pltpu.VMEM)
    formed = pl.pallas_call(
        lambda *refs: form_beams(times, *refs),
        out_shape=jax.ShapeDtypeStruct((beam_count, times, 2, stations, samples), jnp.bfloat16),
        in_specs=[vmem, vmem],
        out_specs=vmem,
        scratch_shapes=[pltpu.VMEM((beam_count, 2, stations, samples), jnp.float32)],
        compiler_params=pltpu.CompilerParams(vmem_limit_bytes=16 * 2**20),
        name="form_beams",
    )(voltages.reshape(stations, samples, width), weights.reshape(stations, 2, beam_count, width // 2))
    formed = formed.reshape(groups * times, 2, stations, samples)
    turned = lax.all_to_all(formed, ("stn", "tchunk"), 0, 0, tiled=True)
    turned = turned.reshape(groups, times, 2, stations, samples)
    row = lax.axis_index("tchunk").astype(jnp.int32).reshape(1)
    all_stations = groups * stations
    result = pl.pallas_call(
        lambda *refs: correlate(1.0 / (samples * times), *refs),
        out_shape=jax.ShapeDtypeStruct((2, all_stations // times, all_stations), jnp.float32),
        in_specs=[pl.BlockSpec(memory_space=pltpu.SMEM), vmem],
        out_specs=vmem,
        compiler_params=pltpu.CompilerParams(vmem_limit_bytes=16 * 2**20),
        name="correlate",
    )(row, turned)
    return result[:, None, None]


def solution(mesh):
    in_specs = (P("stn", "chan", "tchunk", None), P("stn", "chan", None, None, None))
    out_specs = P(None, "chan", "stn", "tchunk", None)
    return jax.shard_map(local, mesh=mesh, in_specs=in_specs, out_specs=out_specs, check_vma=False)
```

```python
import jax
import jax.numpy as jnp
from jax import lax
from jax.experimental import pallas as pl
from jax.experimental.pallas import tpu as pltpu
from jax.sharding import PartitionSpec as P

NT_DIMS = (((1,), (1,)), ((), ()))


def form_beams(copies, pieces, volt_hbm, wgt_hbm, out_ref, volt_ref, wgt_ref, held, sems):
    stations, beam_count = wgt_ref.shape[0], wgt_ref.shape[2]
    step = stations // pieces
    loads = []
    for p in range(pieces):
        part = pl.ds(p * step, step)
        loads.append(
            (
                pltpu.make_async_copy(wgt_hbm.at[part], wgt_ref.at[part], sems.at[0, p]),
                pltpu.make_async_copy(volt_hbm.at[part], volt_ref.at[part], sems.at[1, p]),
            )
        )
    for pair in loads:
        for load in pair:
            load.start()
    for s in range(stations):
        if s % step == 0:
            for load in loads[s // step]:
                load.wait()
        w_re = wgt_ref[s, 0]
        w_im = wgt_ref[s, 1]
        upper = jnp.concatenate([w_re, -w_im], axis=-1)
        lower = jnp.concatenate([w_im, w_re], axis=-1)
        matrix = jnp.concatenate([upper, lower], axis=0)
        formed = lax.dot_general(matrix, volt_ref[s], NT_DIMS, preferred_element_type=jnp.float32)
        held[s] = formed.reshape(held.shape[1:])
    rounded = jnp.transpose(held[...], (2, 1, 0, 3)).astype(jnp.bfloat16)
    for c in range(copies):
        out_ref[:, c] = rounded


def correlate(scale, row_ref, beams_ref, out_ref):
    groups, times = beams_ref.shape[0], beams_ref.shape[1]
    stations, samples = beams_ref.shape[3], beams_ref.shape[4]
    row_groups = out_ref.shape[1] // stations
    first = row_ref[0] * row_groups
    total = None
    for t in range(times):
        re = beams_ref[:, t, 0].reshape(groups * stations, samples)
        im = beams_ref[:, t, 1].reshape(groups * stations, samples)
        left = jnp.concatenate([re, im], axis=-1)
        row_re = beams_ref[pl.ds(first, row_groups), t, 0].reshape(row_groups * stations, samples)
        row_im = beams_ref[pl.ds(first, row_groups), t, 1].reshape(row_groups * stations, samples)
        left_rows = jnp.concatenate([row_re, row_im], axis=-1)
        other_rows = jnp.concatenate([row_im, -row_re], axis=-1)
        rows = jnp.concatenate([left_rows, other_rows], axis=0)
        part = lax.dot_general(rows, left, NT_DIMS, preferred_element_type=jnp.float32)
        total = part if total is None else total + part
    out_ref[...] = (total * scale).reshape(out_ref.shape).astype(out_ref.dtype)


def correlate_rows(row, beams, rows, columns, scale, dtype, name):
    return pl.pallas_call(
        lambda *refs: correlate(scale, *refs),
        out_shape=jax.ShapeDtypeStruct((2, rows, columns), dtype),
        in_specs=[pl.BlockSpec(memory_space=pltpu.SMEM), pl.BlockSpec(memory_space=pltpu.VMEM)],
        out_specs=pl.BlockSpec(memory_space=pltpu.VMEM),
        compiler_params=pltpu.CompilerParams(vmem_limit_bytes=16 * 2**20),
        cost_estimate=pl.CostEstimate(flops=4 * rows * columns * 512, bytes_accessed=2**20, transcendentals=0),
        name=name,
    )(row, beams)


def local(voltages, weights):
    stations, _, samples, width = voltages.shape
    beam_count = weights.shape[3]
    times = lax.axis_size("tchunk")
    groups = lax.axis_size("stn")
    vmem = pl.BlockSpec(memory_space=pltpu.VMEM)
    pieces = 2 if stations % 2 == 0 else 1
    formed = pl.pallas_call(
        lambda *refs: form_beams(times // 2, pieces, *refs),
        out_shape=jax.ShapeDtypeStruct((beam_count, times // 2, 2, stations, samples), jnp.bfloat16),
        in_specs=[pl.BlockSpec(memory_space=pltpu.HBM)] * 2,
        out_specs=vmem,
        scratch_shapes=[
            pltpu.VMEM((stations, samples, width), jnp.bfloat16),
            pltpu.VMEM((stations, 2, beam_count, width // 2), jnp.bfloat16),
            pltpu.VMEM((stations, 2, beam_count, samples), jnp.float32),
            pltpu.SemaphoreType.DMA((2, pieces)),
        ],
        compiler_params=pltpu.CompilerParams(vmem_limit_bytes=16 * 2**20),
        name="form_beams",
    )(
        pltpu.with_memory_space_constraint(voltages.reshape(stations, samples, width), pltpu.HBM),
        pltpu.with_memory_space_constraint(weights.reshape(stations, 2, beam_count, width // 2), pltpu.HBM),
    )
    classes = [[g * times + t for g in range(groups) for t in range(c, times, 2)] for c in range(2)]
    formed = formed.reshape(groups * times // 2, 2, stations, samples)
    turned = lax.all_to_all(formed, ("stn", "tchunk"), 0, 0, axis_index_groups=classes, tiled=True)
    turned = turned.reshape(groups, times // 2, 2, stations, samples)
    row = lax.axis_index("tchunk").astype(jnp.int32).reshape(1)
    columns = groups * stations
    rows = columns // times
    scale = 1.0 / (samples * times)
    theirs = correlate_rows(row ^ 1, turned, rows, columns, scale, jnp.bfloat16, "correlate_theirs")
    arrived = lax.ppermute(theirs, "tchunk", [(t, t ^ 1) for t in range(times)])
    ours = correlate_rows(row, turned, rows, columns, scale, jnp.float32, "correlate_ours")
    return (ours + arrived.astype(jnp.float32))[:, None, None]


def solution(mesh):
    in_specs = (P("stn", "chan", "tchunk", None), P("stn", "chan", None, None, None))
    out_specs = P(None, "chan", "stn", "tchunk", None)
    return jax.shard_map(local, mesh=mesh, in_specs=in_specs, out_specs=out_specs, check_vma=False)
```

```python
import jax
import jax.numpy as jnp
from jax import lax
from jax.experimental import pallas as pl
from jax.experimental.pallas import tpu as pltpu
from jax.sharding import PartitionSpec as P

NT_DIMS = (((1,), (1,)), ((), ()))


def form_beams(copies, pieces, volt_hbm, wgt_hbm, out_ref, volt_ref, wgt_ref, held, sems):
    stations, beam_count = wgt_ref.shape[0], wgt_ref.shape[2]
    step = stations // pieces
    loads = []
    for p in range(pieces):
        part = pl.ds(p * step, step)
        loads.append(
            (
                pltpu.make_async_copy(wgt_hbm.at[part], wgt_ref.at[part], sems.at[0, p]),
                pltpu.make_async_copy(volt_hbm.at[part], volt_ref.at[part], sems.at[1, p]),
            )
        )
    for pair in loads:
        for load in pair:
            load.start()
    for s in range(stations):
        if s % step == 0:
            for load in loads[s // step]:
                load.wait()
        w_re = wgt_ref[s, 0]
        w_im = wgt_ref[s, 1]
        upper = jnp.concatenate([w_re, -w_im], axis=-1)
        lower = jnp.concatenate([w_im, w_re], axis=-1)
        matrix = jnp.concatenate([upper, lower], axis=0)
        formed = lax.dot_general(matrix, volt_ref[s], NT_DIMS, preferred_element_type=jnp.float32)
        held[s] = formed.reshape(held.shape[1:])
    rounded = jnp.transpose(held[...], (2, 1, 0, 3)).astype(jnp.bfloat16)
    for b in range(beam_count):
        for c in range(copies):
            out_ref[b ^ 1, c] = rounded[b]


def correlate(scale, row_ref, beams_ref, out_ref):
    groups, times = beams_ref.shape[0], beams_ref.shape[1]
    stations, samples = beams_ref.shape[3], beams_ref.shape[4]
    row_groups = out_ref.shape[1] // stations
    first = row_ref[0] * row_groups
    total = None
    for t in range(times):
        re = jnp.concatenate([beams_ref[g ^ 1, t, 0] for g in range(groups)], axis=0)
        im = jnp.concatenate([beams_ref[g ^ 1, t, 1] for g in range(groups)], axis=0)
        left = jnp.concatenate([re, im], axis=-1)
        row_re = jnp.concatenate([beams_ref[first + (g ^ 1), t, 0] for g in range(row_groups)], axis=0)
        row_im = jnp.concatenate([beams_ref[first + (g ^ 1), t, 1] for g in range(row_groups)], axis=0)
        left_rows = jnp.concatenate([row_re, row_im], axis=-1)
        other_rows = jnp.concatenate([row_im, -row_re], axis=-1)
        rows = jnp.concatenate([left_rows, other_rows], axis=0)
        part = lax.dot_general(rows, left, NT_DIMS, preferred_element_type=jnp.float32)
        total = part if total is None else total + part
    out_ref[...] = (total * scale).reshape(out_ref.shape).astype(out_ref.dtype)


def correlate_rows(row, beams, rows, columns, scale, dtype, name):
    return pl.pallas_call(
        lambda *refs: correlate(scale, *refs),
        out_shape=jax.ShapeDtypeStruct((2, rows, columns), dtype),
        in_specs=[pl.BlockSpec(memory_space=pltpu.SMEM), pl.BlockSpec(memory_space=pltpu.VMEM)],
        out_specs=pl.BlockSpec(memory_space=pltpu.VMEM),
        compiler_params=pltpu.CompilerParams(vmem_limit_bytes=16 * 2**20),
        cost_estimate=pl.CostEstimate(flops=4 * rows * columns * 512, bytes_accessed=2**20, transcendentals=0),
        name=name,
    )(row, beams)


def local(voltages, weights):
    stations, _, samples, width = voltages.shape
    beam_count = weights.shape[3]
    times = lax.axis_size("tchunk")
    groups = lax.axis_size("stn")
    vmem = pl.BlockSpec(memory_space=pltpu.VMEM)
    pieces = 2 if stations % 2 == 0 else 1
    formed = pl.pallas_call(
        lambda *refs: form_beams(times // 2, pieces, *refs),
        out_shape=jax.ShapeDtypeStruct((beam_count, times // 2, 2, stations, samples), jnp.bfloat16),
        in_specs=[pl.BlockSpec(memory_space=pltpu.HBM)] * 2,
        out_specs=vmem,
        scratch_shapes=[
            pltpu.VMEM((stations, samples, width), jnp.bfloat16),
            pltpu.VMEM((stations, 2, beam_count, width // 2), jnp.bfloat16),
            pltpu.VMEM((stations, 2, beam_count, samples), jnp.float32),
            pltpu.SemaphoreType.DMA((2, pieces)),
        ],
        compiler_params=pltpu.CompilerParams(vmem_limit_bytes=16 * 2**20),
        name="form_beams",
    )(
        pltpu.with_memory_space_constraint(voltages.reshape(stations, samples, width), pltpu.HBM),
        pltpu.with_memory_space_constraint(weights.reshape(stations, 2, beam_count, width // 2), pltpu.HBM),
    )
    classes = [[(g ^ 1) * times + t for g in range(groups) for t in range(c, times, 2)] for c in range(2)]
    formed = formed.reshape(groups * times // 2, 2, stations, samples)
    turned = lax.all_to_all(formed, ("stn", "tchunk"), 0, 0, axis_index_groups=classes, tiled=True)
    turned = turned.reshape(groups, times // 2, 2, stations, samples)
    row = lax.axis_index("tchunk").astype(jnp.int32).reshape(1)
    columns = groups * stations
    rows = columns // times
    scale = 1.0 / (samples * times)
    theirs = correlate_rows(row ^ 1, turned, rows, columns, scale, jnp.bfloat16, "correlate_theirs")
    arrived = lax.ppermute(theirs, "tchunk", [(t, t ^ 1) for t in range(times)])
    ours = correlate_rows(row, turned, rows, columns, scale, jnp.float32, "correlate_ours")
    return (ours + arrived.astype(jnp.float32))[:, None, None]


def solution(mesh):
    in_specs = (P("stn", "chan", "tchunk", None), P("stn", "chan", None, None, None))
    out_specs = P(None, "chan", "stn", "tchunk", None)
    return jax.shard_map(local, mesh=mesh, in_specs=in_specs, out_specs=out_specs, check_vma=False)
```

```python
import jax
import jax.numpy as jnp
from jax import lax
from jax.experimental import pallas as pl
from jax.experimental.pallas import tpu as pltpu
from jax.sharding import PartitionSpec as P

NT_DIMS = (((1,), (1,)), ((), ()))


def form_beams(copies, pieces, volt_hbm, wgt_hbm, out_ref, volt_ref, wgt_ref, held, sems):
    stations, beam_count = wgt_ref.shape[0], wgt_ref.shape[2]
    step = stations // pieces
    loads = []
    for p in range(pieces):
        part = pl.ds(p * step, step)
        loads.append(
            (
                pltpu.make_async_copy(wgt_hbm.at[part], wgt_ref.at[part], sems.at[0, p]),
                pltpu.make_async_copy(volt_hbm.at[part], volt_ref.at[part], sems.at[1, p]),
            )
        )
    for pair in loads:
        for load in pair:
            load.start()
    for s in range(stations):
        if s % step == 0:
            for load in loads[s // step]:
                load.wait()
        w_re = wgt_ref[s, 0]
        w_im = wgt_ref[s, 1]
        upper = jnp.concatenate([w_re, -w_im], axis=-1)
        lower = jnp.concatenate([w_im, w_re], axis=-1)
        matrix = jnp.concatenate([upper, lower], axis=0)
        formed = lax.dot_general(matrix, volt_ref[s], NT_DIMS, preferred_element_type=jnp.float32)
        held[s] = formed.reshape(held.shape[1:])
    rounded = jnp.transpose(held[...], (2, 1, 0, 3)).astype(jnp.bfloat16)
    for b in range(beam_count):
        for c in range(copies):
            out_ref[b ^ 1, c] = rounded[b]


def correlate(scale, packed, row_ref, beams_ref, *out_refs):
    groups, times = beams_ref.shape[0], beams_ref.shape[1]
    row_count = out_refs[0].shape[0]
    row_groups = row_count // beams_ref.shape[3]
    first = row_ref[0] * row_groups
    order = [lax.rem(first + (g ^ 1), groups) for g in range(groups)]
    total = None
    for t in range(times):
        re = [beams_ref[g, t, 0] for g in order]
        im = [beams_ref[g, t, 1] for g in order]
        left = jnp.concatenate([jnp.concatenate(re, axis=0), jnp.concatenate(im, axis=0)], axis=-1)
        row_re = jnp.concatenate(re[:row_groups], axis=0)
        row_im = jnp.concatenate(im[:row_groups], axis=0)
        left_rows = jnp.concatenate([row_re, row_im], axis=-1)
        other_rows = jnp.concatenate([row_im, -row_re], axis=-1)
        rows = jnp.concatenate([left_rows, other_rows], axis=0)
        part = lax.dot_general(rows, left, NT_DIMS, preferred_element_type=jnp.float32)
        total = part if total is None else total + part
    total = total * scale
    re, im = total[:row_count], total[row_count:]
    if packed:
        upper, _ = triangles(row_count)
        diagonal = jnp.where(upper, re[:, :row_count], im[:, :row_count])
        out_refs[0][:, :row_count] = diagonal.astype(out_refs[0].dtype)
        out_refs[0][:, row_count:] = re[:, row_count:].astype(out_refs[0].dtype)
        out_refs[1][...] = im[:, row_count:].astype(out_refs[1].dtype)
    else:
        out_refs[0][...] = re.astype(out_refs[0].dtype)
        out_refs[1][...] = im.astype(out_refs[1].dtype)


def triangles(size):
    i = lax.broadcasted_iota(jnp.int32, (size, size), 0)
    j = lax.broadcasted_iota(jnp.int32, (size, size), 1)
    return i <= j, i > j


def correlate_rows(row, beams, rows, columns, scale, packed, dtype, name):
    second = columns - rows if packed else columns
    return pl.pallas_call(
        lambda *refs: correlate(scale, packed, *refs),
        out_shape=[jax.ShapeDtypeStruct((rows, columns), dtype), jax.ShapeDtypeStruct((rows, second), dtype)],
        in_specs=[pl.BlockSpec(memory_space=pltpu.SMEM), pl.BlockSpec(memory_space=pltpu.VMEM)],
        out_specs=[pl.BlockSpec(memory_space=pltpu.VMEM)] * 2,
        compiler_params=pltpu.CompilerParams(vmem_limit_bytes=16 * 2**20),
        cost_estimate=pl.CostEstimate(flops=4 * rows * columns * 512, bytes_accessed=2**20, transcendentals=0),
        name=name,
    )(row, beams)


def add_rows(part, row_ref, ours_ref, *refs):
    out_hbm, total, sems = refs[-3:]
    rows, columns = total.shape
    blocks = columns // rows
    both = refs[0][:, :rows].astype(jnp.float32)
    mirrored = both.T
    upper, lower = triangles(rows)
    stores = []
    for k in list(range(1, blocks)) + [0]:
        at = pl.ds(k * rows, rows)
        if k == 0:
            if part == 0:
                block = jnp.where(upper, both, mirrored)
            else:
                block = jnp.where(lower, both, 0.0) - jnp.where(lower, both, 0.0).T
        elif part == 0:
            block = refs[0][:, at].astype(jnp.float32)
        else:
            block = refs[1][:, pl.ds((k - 1) * rows, rows)].astype(jnp.float32)
        total[:, at] = ours_ref[:, at] + block
        place = pl.multiple_of(lax.rem(row_ref[0] + k, blocks) * rows, rows)
        stores.append(pltpu.make_async_copy(total.at[:, at], out_hbm.at[part, :, pl.ds(place, rows)], sems.at[k]))
        stores[-1].start()
    for store in stores:
        store.wait()


def add_part(part, row, ours, arrived, result):
    rows, columns = ours.shape
    vmem = pl.BlockSpec(memory_space=pltpu.VMEM)
    hbm = pl.BlockSpec(memory_space=pltpu.HBM)
    return pl.pallas_call(
        lambda *refs: add_rows(part, *refs),
        out_shape=jax.ShapeDtypeStruct((2, rows, columns), jnp.float32),
        in_specs=[pl.BlockSpec(memory_space=pltpu.SMEM), vmem] + [vmem] * len(arrived) + [hbm] * len(result),
        out_specs=hbm,
        scratch_shapes=[pltpu.VMEM((rows, columns), jnp.float32), pltpu.SemaphoreType.DMA((columns // rows,))],
        input_output_aliases={2 + len(arrived): 0} if result else {},
        compiler_params=pltpu.CompilerParams(vmem_limit_bytes=16 * 2**20),
        cost_estimate=pl.CostEstimate(flops=rows * columns, bytes_accessed=8 * rows * columns, transcendentals=0),
        name="add_re" if part == 0 else "add_im",
    )(row, ours, *arrived, *result)


def local(voltages, weights):
    stations, _, samples, width = voltages.shape
    beam_count = weights.shape[3]
    times = lax.axis_size("tchunk")
    groups = lax.axis_size("stn")
    vmem = pl.BlockSpec(memory_space=pltpu.VMEM)
    pieces = 2 if stations % 2 == 0 else 1
    formed = pl.pallas_call(
        lambda *refs: form_beams(times // 2, pieces, *refs),
        out_shape=jax.ShapeDtypeStruct((beam_count, times // 2, 2, stations, samples), jnp.bfloat16),
        in_specs=[pl.BlockSpec(memory_space=pltpu.HBM)] * 2,
        out_specs=vmem,
        scratch_shapes=[
            pltpu.VMEM((stations, samples, width), jnp.bfloat16),
            pltpu.VMEM((stations, 2, beam_count, width // 2), jnp.bfloat16),
            pltpu.VMEM((stations, 2, beam_count, samples), jnp.float32),
            pltpu.SemaphoreType.DMA((2, pieces)),
        ],
        compiler_params=pltpu.CompilerParams(vmem_limit_bytes=16 * 2**20),
        name="form_beams",
    )(
        pltpu.with_memory_space_constraint(voltages.reshape(stations, samples, width), pltpu.HBM),
        pltpu.with_memory_space_constraint(weights.reshape(stations, 2, beam_count, width // 2), pltpu.HBM),
    )
    classes = [[(g ^ 1) * times + t for g in range(groups) for t in range(c, times, 2)] for c in range(2)]
    formed = formed.reshape(groups * times // 2, 2, stations, samples)
    turned = lax.all_to_all(formed, ("stn", "tchunk"), 0, 0, axis_index_groups=classes, tiled=True)
    turned = turned.reshape(groups, times // 2, 2, stations, samples)
    row = lax.axis_index("tchunk").astype(jnp.int32).reshape(1)
    columns = groups * stations
    rows = columns // times
    scale = 1.0 / (samples * times)
    theirs = correlate_rows(row ^ 1, turned, rows, columns, scale, True, jnp.bfloat16, "correlate_theirs")
    swap = [(t, t ^ 1) for t in range(times)]
    arrived = [lax.ppermute(part, "tchunk", swap) for part in theirs]
    ours = correlate_rows(row, turned, rows, columns, scale, False, jnp.float32, "correlate_ours")
    result = add_part(0, row, ours[0], arrived[:1], [])
    result = add_part(1, row, ours[1], arrived, [result])
    return result[:, None, None]


def solution(mesh):
    in_specs = (P("stn", "chan", "tchunk", None), P("stn", "chan", None, None, None))
    out_specs = P(None, "chan", "stn", "tchunk", None)
    return jax.shard_map(local, mesh=mesh, in_specs=in_specs, out_specs=out_specs, check_vma=False)
```

```python
import jax
import jax.numpy as jnp
from jax import lax
from jax.experimental import pallas as pl
from jax.experimental.pallas import tpu as pltpu
from jax.sharding import PartitionSpec as P

NT_DIMS = (((1,), (1,)), ((), ()))
LAST = 2


def form_beams(copies, pieces, volt_hbm, wgt_hbm, out_ref, volt_ref, wgt_ref, held, sems):
    stations, beam_count = wgt_ref.shape[0], wgt_ref.shape[2]
    step = stations // pieces
    loads = []
    for p in range(pieces):
        part = pl.ds(p * step, step)
        loads.append(
            (
                pltpu.make_async_copy(wgt_hbm.at[part], wgt_ref.at[part], sems.at[0, p]),
                pltpu.make_async_copy(volt_hbm.at[part], volt_ref.at[part], sems.at[1, p]),
            )
        )
    for pair in loads:
        for load in pair:
            load.start()
    for s in range(stations):
        if s % step == 0:
            for load in loads[s // step]:
                load.wait()
        w_re = wgt_ref[s, 0]
        w_im = wgt_ref[s, 1]
        upper = jnp.concatenate([w_re, -w_im], axis=-1)
        lower = jnp.concatenate([w_im, w_re], axis=-1)
        matrix = jnp.concatenate([upper, lower], axis=0)
        formed = lax.dot_general(matrix, volt_ref[s], NT_DIMS, preferred_element_type=jnp.float32)
        held[s] = formed.reshape(held.shape[1:])
    rounded = jnp.transpose(held[...], (2, 1, 0, 3)).astype(jnp.bfloat16)
    for b in range(beam_count):
        for c in range(copies):
            out_ref[b ^ 1, c] = rounded[b]


def correlate(scale, packed, row_ref, beams_ref, *out_refs):
    groups, times = beams_ref.shape[0], beams_ref.shape[1]
    row_count, columns = out_refs[0].shape[0], groups * beams_ref.shape[3]
    row_groups = row_count // beams_ref.shape[3]
    first = row_ref[0] * row_groups
    order = [lax.rem(first + (g ^ 1), groups) for g in range(groups)]
    total = None
    for t in range(times):
        re = [beams_ref[g, t, 0] for g in order]
        im = [beams_ref[g, t, 1] for g in order]
        left = jnp.concatenate([jnp.concatenate(re, axis=0), jnp.concatenate(im, axis=0)], axis=-1)
        row_re = jnp.concatenate(re[:row_groups], axis=0)
        row_im = jnp.concatenate(im[:row_groups], axis=0)
        left_rows = jnp.concatenate([row_re, row_im], axis=-1)
        other_rows = jnp.concatenate([row_im, -row_re], axis=-1)
        rows = jnp.concatenate([left_rows, other_rows], axis=0)
        part = lax.dot_general(rows, left, NT_DIMS, preferred_element_type=jnp.float32)
        total = part if total is None else total + part
    total = total * scale
    re, im = total[:row_count], total[row_count:]
    if packed:
        upper, _ = triangles(row_count)
        diagonal = jnp.where(upper, re[:, :row_count], im[:, :row_count])
        for (part, k), (to, at) in places(columns // row_count, row_count).items():
            block = (re, im)[part][:, k * row_count : (k + 1) * row_count]
            if k == 0:
                block = diagonal
            out_refs[to][:, at] = block.astype(out_refs[to].dtype)
    else:
        out_refs[0][...] = re.astype(out_refs[0].dtype)
        out_refs[1][...] = im.astype(out_refs[1].dtype)


def places(blocks, size):
    order = [(0, k) for k in range(blocks)] + [(1, k) for k in range(1, blocks)]
    first = len(order) - LAST
    return {b: (int(n >= first), slice((n % first) * size, (n % first + 1) * size)) for n, b in enumerate(order)}


def triangles(size):
    i = lax.broadcasted_iota(jnp.int32, (size, size), 0)
    j = lax.broadcasted_iota(jnp.int32, (size, size), 1)
    return i <= j, i > j


def correlate_rows(row, beams, rows, columns, scale, packed, dtype, name):
    widths = (2 * columns - (1 + LAST) * rows, LAST * rows) if packed else (columns, columns)
    return pl.pallas_call(
        lambda *refs: correlate(scale, packed, *refs),
        out_shape=[jax.ShapeDtypeStruct((rows, width), dtype) for width in widths],
        in_specs=[pl.BlockSpec(memory_space=pltpu.SMEM), pl.BlockSpec(memory_space=pltpu.VMEM)],
        out_specs=[pl.BlockSpec(memory_space=pltpu.VMEM)] * 2,
        compiler_params=pltpu.CompilerParams(vmem_limit_bytes=16 * 2**20),
        cost_estimate=pl.CostEstimate(flops=4 * rows * columns * 512, bytes_accessed=2**20, transcendentals=0),
        name=name,
    )(row, beams)


def add_rows(stage, row_ref, re_ref, im_ref, arrived_ref, *refs):
    out_hbm, total, sems = refs[-3:]
    rows, columns = re_ref.shape
    blocks = columns // rows
    here = [(b, at) for b, (to, at) in places(blocks, rows).items() if to == stage and b[1] > 0]
    if stage == 0:
        both = arrived_ref[:, :rows].astype(jnp.float32)
        upper, lower = triangles(rows)
        strict = jnp.where(lower, both, 0.0)
        here += [((0, 0), jnp.where(upper, both, both.T)), ((1, 0), strict - strict.T)]
    stores = []
    for n, ((part, k), block) in enumerate(here):
        if k > 0:
            block = arrived_ref[:, block].astype(jnp.float32)
        total[n] = (re_ref, im_ref)[part][:, k * rows : (k + 1) * rows] + block
        place = pl.multiple_of(lax.rem(row_ref[0] + k, blocks) * rows, rows)
        stores.append(pltpu.make_async_copy(total.at[n], out_hbm.at[part, :, pl.ds(place, rows)], sems.at[n]))
        stores[-1].start()
    for store in stores:
        store.wait()


def add_part(stage, row, ours, arrived, result):
    rows, columns = ours[0].shape
    vmem = pl.BlockSpec(memory_space=pltpu.VMEM)
    hbm = pl.BlockSpec(memory_space=pltpu.HBM)
    count = LAST if stage else 2 * (columns // rows) - LAST
    return pl.pallas_call(
        lambda *refs: add_rows(stage, *refs),
        out_shape=jax.ShapeDtypeStruct((2, rows, columns), jnp.float32),
        in_specs=[pl.BlockSpec(memory_space=pltpu.SMEM), vmem, vmem, vmem] + [hbm] * len(result),
        out_specs=hbm,
        scratch_shapes=[pltpu.VMEM((count, rows, rows), jnp.float32), pltpu.SemaphoreType.DMA((count,))],
        input_output_aliases={4: 0} if result else {},
        compiler_params=pltpu.CompilerParams(vmem_limit_bytes=16 * 2**20),
        cost_estimate=pl.CostEstimate(flops=rows * columns, bytes_accessed=8 * rows * columns, transcendentals=0),
        name="add_last" if stage else "add_first",
    )(row, *ours, arrived, *result)


def local(voltages, weights):
    stations, _, samples, width = voltages.shape
    beam_count = weights.shape[3]
    times = lax.axis_size("tchunk")
    groups = lax.axis_size("stn")
    vmem = pl.BlockSpec(memory_space=pltpu.VMEM)
    pieces = 2 if stations % 2 == 0 else 1
    formed = pl.pallas_call(
        lambda *refs: form_beams(times // 2, pieces, *refs),
        out_shape=jax.ShapeDtypeStruct((beam_count, times // 2, 2, stations, samples), jnp.bfloat16),
        in_specs=[pl.BlockSpec(memory_space=pltpu.HBM)] * 2,
        out_specs=vmem,
        scratch_shapes=[
            pltpu.VMEM((stations, samples, width), jnp.bfloat16),
            pltpu.VMEM((stations, 2, beam_count, width // 2), jnp.bfloat16),
            pltpu.VMEM((stations, 2, beam_count, samples), jnp.float32),
            pltpu.SemaphoreType.DMA((2, pieces)),
        ],
        compiler_params=pltpu.CompilerParams(vmem_limit_bytes=16 * 2**20),
        name="form_beams",
    )(
        pltpu.with_memory_space_constraint(voltages.reshape(stations, samples, width), pltpu.HBM),
        pltpu.with_memory_space_constraint(weights.reshape(stations, 2, beam_count, width // 2), pltpu.HBM),
    )
    classes = [[(g ^ 1) * times + t for g in range(groups) for t in range(c, times, 2)] for c in range(2)]
    formed = formed.reshape(groups * times // 2, 2, stations, samples)
    turned = lax.all_to_all(formed, ("stn", "tchunk"), 0, 0, axis_index_groups=classes, tiled=True)
    turned = turned.reshape(groups, times // 2, 2, stations, samples)
    row = lax.axis_index("tchunk").astype(jnp.int32).reshape(1)
    columns = groups * stations
    rows = columns // times
    scale = 1.0 / (samples * times)
    theirs = correlate_rows(row ^ 1, turned, rows, columns, scale, True, jnp.bfloat16, "correlate_theirs")
    swap = [(t, t ^ 1) for t in range(times)]
    arrived = [lax.ppermute(part, "tchunk", swap) for part in theirs]
    ours = correlate_rows(row, turned, rows, columns, scale, False, jnp.float32, "correlate_ours")
    result = add_part(0, row, ours, arrived[0], [])
    result = add_part(1, row, ours, arrived[1], [result])
    return result[:, None, None]


def solution(mesh):
    in_specs = (P("stn", "chan", "tchunk", None), P("stn", "chan", None, None, None))
    out_specs = P(None, "chan", "stn", "tchunk", None)
    return jax.shard_map(local, mesh=mesh, in_specs=in_specs, out_specs=out_specs, check_vma=False)
```

```python
import jax
import jax.numpy as jnp
from jax import lax
from jax.experimental import pallas as pl
from jax.experimental.pallas import tpu as pltpu
from jax.sharding import PartitionSpec as P

NT_DIMS = (((1,), (1,)), ((), ()))


def form_beams(copies, pieces, volt_hbm, wgt_hbm, out_ref, volt_ref, wgt_ref, held, sems):
    stations, beam_count = wgt_ref.shape[0], wgt_ref.shape[2]
    step = stations // pieces
    loads = []
    for p in range(pieces):
        part = pl.ds(p * step, step)
        loads.append(
            (
                pltpu.make_async_copy(wgt_hbm.at[part], wgt_ref.at[part], sems.at[0, p]),
                pltpu.make_async_copy(volt_hbm.at[part], volt_ref.at[part], sems.at[1, p]),
            )
        )
    for pair in loads:
        for load in pair:
            load.start()
    for s in range(stations):
        if s % step == 0:
            for load in loads[s // step]:
                load.wait()
        w_re = wgt_ref[s, 0]
        w_im = wgt_ref[s, 1]
        upper = jnp.concatenate([w_re, -w_im], axis=-1)
        lower = jnp.concatenate([w_im, w_re], axis=-1)
        matrix = jnp.concatenate([upper, lower], axis=0)
        formed = lax.dot_general(matrix, volt_ref[s], NT_DIMS, preferred_element_type=jnp.float32)
        held[s] = formed.reshape(held.shape[1:])
    rounded = jnp.transpose(held[...], (2, 1, 0, 3)).astype(jnp.bfloat16)
    for b in range(beam_count):
        for c in range(copies):
            out_ref[b ^ 1, c] = rounded[b]


def correlate(scale, packed, row_ref, beams_ref, *out_refs):
    groups, times = beams_ref.shape[0], beams_ref.shape[1]
    row_count, columns = out_refs[0].shape[0], groups * beams_ref.shape[3]
    row_groups = row_count // beams_ref.shape[3]
    first = row_ref[0] * row_groups
    order = [lax.rem(first + (g ^ 1), groups) for g in range(groups)]
    total = None
    for t in range(times):
        re = [beams_ref[g, t, 0] for g in order]
        im = [beams_ref[g, t, 1] for g in order]
        left = jnp.concatenate([jnp.concatenate(re, axis=0), jnp.concatenate(im, axis=0)], axis=-1)
        row_re = jnp.concatenate(re[:row_groups], axis=0)
        row_im = jnp.concatenate(im[:row_groups], axis=0)
        left_rows = jnp.concatenate([row_re, row_im], axis=-1)
        other_rows = jnp.concatenate([row_im, -row_re], axis=-1)
        rows = jnp.concatenate([left_rows, other_rows], axis=0)
        part = lax.dot_general(rows, left, NT_DIMS, preferred_element_type=jnp.float32)
        total = part if total is None else total + part
    total = total * scale
    re, im = total[:row_count], total[row_count:]
    if packed:
        upper, _ = triangles(row_count)
        diagonal = jnp.where(upper, re[:, :row_count], im[:, :row_count])
        for (part, k), at in places(columns // row_count, row_count).items():
            block = (re, im)[part][:, k * row_count : (k + 1) * row_count]
            if k == 0:
                block = diagonal
            out_refs[0][:, at] = block.astype(out_refs[0].dtype)
    else:
        out_refs[0][...] = re.astype(out_refs[0].dtype)
        out_refs[1][...] = im.astype(out_refs[1].dtype)


def places(blocks, size):
    order = [(0, k) for k in range(blocks)] + [(1, k) for k in range(1, blocks)]
    return {b: slice(n * size, (n + 1) * size) for n, b in enumerate(order)}


def triangles(size):
    i = lax.broadcasted_iota(jnp.int32, (size, size), 0)
    j = lax.broadcasted_iota(jnp.int32, (size, size), 1)
    return i <= j, i > j


def correlate_rows(row, beams, rows, columns, scale, packed, dtype, name):
    widths = (2 * columns - rows,) if packed else (columns, columns)
    return pl.pallas_call(
        lambda *refs: correlate(scale, packed, *refs),
        out_shape=[jax.ShapeDtypeStruct((rows, width), dtype) for width in widths],
        in_specs=[pl.BlockSpec(memory_space=pltpu.SMEM), pl.BlockSpec(memory_space=pltpu.VMEM)],
        out_specs=[pl.BlockSpec(memory_space=pltpu.VMEM)] * len(widths),
        compiler_params=pltpu.CompilerParams(vmem_limit_bytes=16 * 2**20),
        cost_estimate=pl.CostEstimate(flops=4 * rows * columns * 512, bytes_accessed=2**20, transcendentals=0),
        name=name,
    )(row, beams)


def add_rows(row_ref, re_ref, im_ref, *refs):
    out_hbm, total, sems = refs[-3:]
    arrived_refs = refs[:-3]
    rows, columns = re_ref.shape
    blocks = columns // rows
    both = arrived_refs[0][:, :rows].astype(jnp.float32)
    upper, lower = triangles(rows)
    strict = jnp.where(lower, both, 0.0)
    here = [(b, at) for b, at in places(blocks, rows).items() if b[1] > 0]
    here += [((0, 0), jnp.where(upper, both, both.T)), ((1, 0), strict - strict.T)]
    stores = []
    for n, ((part, k), block) in enumerate(here):
        if k > 0:
            block = arrived_refs[0][:, block].astype(jnp.float32)
        total[n] = (re_ref, im_ref)[part][:, k * rows : (k + 1) * rows] + block
        place = pl.multiple_of(lax.rem(row_ref[0] + k, blocks) * rows, rows)
        stores.append(pltpu.make_async_copy(total.at[n], out_hbm.at[part, :, pl.ds(place, rows)], sems.at[n]))
        stores[-1].start()
    for store in stores:
        store.wait()


def add_parts(row, ours, arrived):
    rows, columns = ours[0].shape
    vmem = pl.BlockSpec(memory_space=pltpu.VMEM)
    count = 2 * (columns // rows)
    return pl.pallas_call(
        add_rows,
        out_shape=jax.ShapeDtypeStruct((2, rows, columns), jnp.float32),
        in_specs=[pl.BlockSpec(memory_space=pltpu.SMEM)] + [vmem] * (2 + len(arrived)),
        out_specs=pl.BlockSpec(memory_space=pltpu.HBM),
        scratch_shapes=[pltpu.VMEM((count, rows, rows), jnp.float32), pltpu.SemaphoreType.DMA((count,))],
        compiler_params=pltpu.CompilerParams(vmem_limit_bytes=16 * 2**20),
        cost_estimate=pl.CostEstimate(flops=rows * columns, bytes_accessed=8 * rows * columns, transcendentals=0),
        name="add_parts",
    )(row, *ours, *arrived)


def local(voltages, weights):
    stations, _, samples, width = voltages.shape
    beam_count = weights.shape[3]
    times = lax.axis_size("tchunk")
    groups = lax.axis_size("stn")
    vmem = pl.BlockSpec(memory_space=pltpu.VMEM)
    pieces = 2 if stations % 2 == 0 else 1
    formed = pl.pallas_call(
        lambda *refs: form_beams(times // 2, pieces, *refs),
        out_shape=jax.ShapeDtypeStruct((beam_count, times // 2, 2, stations, samples), jnp.bfloat16),
        in_specs=[pl.BlockSpec(memory_space=pltpu.HBM)] * 2,
        out_specs=vmem,
        scratch_shapes=[
            pltpu.VMEM((stations, samples, width), jnp.bfloat16),
            pltpu.VMEM((stations, 2, beam_count, width // 2), jnp.bfloat16),
            pltpu.VMEM((stations, 2, beam_count, samples), jnp.float32),
            pltpu.SemaphoreType.DMA((2, pieces)),
        ],
        compiler_params=pltpu.CompilerParams(vmem_limit_bytes=16 * 2**20),
        name="form_beams",
    )(
        pltpu.with_memory_space_constraint(voltages.reshape(stations, samples, width), pltpu.HBM),
        pltpu.with_memory_space_constraint(weights.reshape(stations, 2, beam_count, width // 2), pltpu.HBM),
    )
    classes = [[(g ^ 1) * times + t for g in range(groups) for t in range(c, times, 2)] for c in range(2)]
    formed = formed.reshape(groups * times // 2, 2, stations, samples)
    turned = lax.all_to_all(formed, ("stn", "tchunk"), 0, 0, axis_index_groups=classes, tiled=True)
    turned = turned.reshape(groups, times // 2, 2, stations, samples)
    row = lax.axis_index("tchunk").astype(jnp.int32).reshape(1)
    columns = groups * stations
    rows = columns // times
    scale = 1.0 / (samples * times)
    theirs = correlate_rows(row ^ 1, turned, rows, columns, scale, True, jnp.bfloat16, "correlate_theirs")
    swap = [(t, t ^ 1) for t in range(times)]
    arrived = [lax.ppermute(part, "tchunk", swap) for part in theirs]
    ours = correlate_rows(row, turned, rows, columns, scale, False, jnp.float32, "correlate_ours")
    result = add_parts(row, ours, arrived)
    return result[:, None, None]


def solution(mesh):
    in_specs = (P("stn", "chan", "tchunk", None), P("stn", "chan", None, None, None))
    out_specs = P(None, "chan", "stn", "tchunk", None)
    return jax.shard_map(local, mesh=mesh, in_specs=in_specs, out_specs=out_specs, check_vma=False)
```

```python
import jax
import jax.numpy as jnp
from jax import lax
from jax.experimental import pallas as pl
from jax.experimental.pallas import tpu as pltpu
from jax.sharding import PartitionSpec as P

NT_DIMS = (((1,), (1,)), ((), ()))


def form_beams(copies, pieces, volt_hbm, wgt_hbm, out_ref, volt_ref, wgt_ref, held, sems):
    stations, beam_count = wgt_ref.shape[0], wgt_ref.shape[2]
    step = stations // pieces
    loads = []
    for p in range(pieces):
        part = pl.ds(p * step, step)
        loads.append(
            (
                pltpu.make_async_copy(wgt_hbm.at[part], wgt_ref.at[part], sems.at[0, p]),
                pltpu.make_async_copy(volt_hbm.at[part], volt_ref.at[part], sems.at[1, p]),
            )
        )
    for pair in loads:
        for load in pair:
            load.start()
    for s in range(0, stations, 2):
        if s % step == 0:
            for load in loads[s // step]:
                load.wait()
        matrices = []
        for q in (s, s + 1):
            w_re = wgt_ref[q, 0]
            w_im = wgt_ref[q, 1]
            matrices += [jnp.concatenate([w_re, -w_im], axis=-1), jnp.concatenate([w_im, w_re], axis=-1)]
        samples = volt_ref.shape[1]
        both = volt_ref[s : s + 2].reshape(2 * samples, volt_ref.shape[2])
        formed = lax.dot_general(jnp.concatenate(matrices, axis=0), both, NT_DIMS, preferred_element_type=jnp.float32)
        half = formed.shape[0] // 2
        held[s] = formed[:half, :samples].reshape(held.shape[1:])
        held[s + 1] = formed[half:, samples:].reshape(held.shape[1:])
    rounded = jnp.transpose(held[...], (2, 1, 0, 3)).astype(jnp.bfloat16)
    for b in range(beam_count):
        for c in range(copies):
            out_ref[b ^ 1, c] = rounded[b]


def correlate(scale, packed, row_ref, beams_ref, *out_refs):
    groups, times = beams_ref.shape[0], beams_ref.shape[1]
    row_count, columns = out_refs[0].shape[0], groups * beams_ref.shape[3]
    row_groups = row_count // beams_ref.shape[3]
    first = row_ref[0] * row_groups
    order = [lax.rem(first + (g ^ 1), groups) for g in range(groups)]
    total = None
    for t in range(times):
        re = [beams_ref[g, t, 0] for g in order]
        im = [beams_ref[g, t, 1] for g in order]
        left = jnp.concatenate([jnp.concatenate(re, axis=0), jnp.concatenate(im, axis=0)], axis=-1)
        row_re = jnp.concatenate(re[:row_groups], axis=0)
        row_im = jnp.concatenate(im[:row_groups], axis=0)
        left_rows = jnp.concatenate([row_re, row_im], axis=-1)
        other_rows = jnp.concatenate([row_im, -row_re], axis=-1)
        rows = jnp.concatenate([left_rows, other_rows], axis=0)
        part = lax.dot_general(rows, left, NT_DIMS, preferred_element_type=jnp.float32)
        total = part if total is None else total + part
    total = total * scale
    re, im = total[:row_count], total[row_count:]
    if packed:
        upper, _ = triangles(row_count)
        diagonal = jnp.where(upper, re[:, :row_count], im[:, :row_count])
        for (part, k), at in places(columns // row_count, row_count).items():
            block = (re, im)[part][:, k * row_count : (k + 1) * row_count]
            if k == 0:
                block = diagonal
            out_refs[0][:, at] = block.astype(out_refs[0].dtype)
    else:
        out_refs[0][...] = re.astype(out_refs[0].dtype)
        out_refs[1][...] = im.astype(out_refs[1].dtype)


def places(blocks, size):
    order = [(0, k) for k in range(blocks)] + [(1, k) for k in range(1, blocks)]
    return {b: slice(n * size, (n + 1) * size) for n, b in enumerate(order)}


def triangles(size):
    i = lax.broadcasted_iota(jnp.int32, (size, size), 0)
    j = lax.broadcasted_iota(jnp.int32, (size, size), 1)
    return i <= j, i > j


def correlate_rows(row, beams, rows, columns, scale, packed, dtype, name):
    widths = (2 * columns - rows,) if packed else (columns, columns)
    return pl.pallas_call(
        lambda *refs: correlate(scale, packed, *refs),
        out_shape=[jax.ShapeDtypeStruct((rows, width), dtype) for width in widths],
        in_specs=[pl.BlockSpec(memory_space=pltpu.SMEM), pl.BlockSpec(memory_space=pltpu.VMEM)],
        out_specs=[pl.BlockSpec(memory_space=pltpu.VMEM)] * len(widths),
        compiler_params=pltpu.CompilerParams(vmem_limit_bytes=16 * 2**20),
        cost_estimate=pl.CostEstimate(flops=4 * rows * columns * 512, bytes_accessed=2**20, transcendentals=0),
        name=name,
    )(row, beams)


def add_rows(row_ref, re_ref, im_ref, *refs):
    out_hbm, total, sems = refs[-3:]
    arrived_refs = refs[:-3]
    rows, columns = re_ref.shape
    blocks = columns // rows
    both = arrived_refs[0][:, :rows].astype(jnp.float32)
    upper, lower = triangles(rows)
    strict = jnp.where(lower, both, 0.0)
    here = [(b, at) for b, at in places(blocks, rows).items() if b[1] > 0]
    here += [((0, 0), jnp.where(upper, both, both.T)), ((1, 0), strict - strict.T)]
    stores = []
    for n, ((part, k), block) in enumerate(here):
        if k > 0:
            block = arrived_refs[0][:, block].astype(jnp.float32)
        total[n] = (re_ref, im_ref)[part][:, k * rows : (k + 1) * rows] + block
        place = pl.multiple_of(lax.rem(row_ref[0] + k, blocks) * rows, rows)
        stores.append(pltpu.make_async_copy(total.at[n], out_hbm.at[part, :, pl.ds(place, rows)], sems.at[n]))
        stores[-1].start()
    for store in stores:
        store.wait()


def add_parts(row, ours, arrived):
    rows, columns = ours[0].shape
    vmem = pl.BlockSpec(memory_space=pltpu.VMEM)
    count = 2 * (columns // rows)
    return pl.pallas_call(
        add_rows,
        out_shape=jax.ShapeDtypeStruct((2, rows, columns), jnp.float32),
        in_specs=[pl.BlockSpec(memory_space=pltpu.SMEM)] + [vmem] * (2 + len(arrived)),
        out_specs=pl.BlockSpec(memory_space=pltpu.HBM),
        scratch_shapes=[pltpu.VMEM((count, rows, rows), jnp.float32), pltpu.SemaphoreType.DMA((count,))],
        compiler_params=pltpu.CompilerParams(vmem_limit_bytes=16 * 2**20),
        cost_estimate=pl.CostEstimate(flops=rows * columns, bytes_accessed=8 * rows * columns, transcendentals=0),
        name="add_parts",
    )(row, *ours, *arrived)


def local(voltages, weights):
    stations, _, samples, width = voltages.shape
    beam_count = weights.shape[3]
    times = lax.axis_size("tchunk")
    groups = lax.axis_size("stn")
    vmem = pl.BlockSpec(memory_space=pltpu.VMEM)
    pieces = 2 if stations % 2 == 0 else 1
    formed = pl.pallas_call(
        lambda *refs: form_beams(times // 2, pieces, *refs),
        out_shape=jax.ShapeDtypeStruct((beam_count, times // 2, 2, stations, samples), jnp.bfloat16),
        in_specs=[pl.BlockSpec(memory_space=pltpu.HBM)] * 2,
        out_specs=vmem,
        scratch_shapes=[
            pltpu.VMEM((stations, samples, width), jnp.bfloat16),
            pltpu.VMEM((stations, 2, beam_count, width // 2), jnp.bfloat16),
            pltpu.VMEM((stations, 2, beam_count, samples), jnp.float32),
            pltpu.SemaphoreType.DMA((2, pieces)),
        ],
        compiler_params=pltpu.CompilerParams(vmem_limit_bytes=16 * 2**20),
        name="form_beams",
    )(
        pltpu.with_memory_space_constraint(voltages.reshape(stations, samples, width), pltpu.HBM),
        pltpu.with_memory_space_constraint(weights.reshape(stations, 2, beam_count, width // 2), pltpu.HBM),
    )
    classes = [[(g ^ 1) * times + t for g in range(groups) for t in range(c, times, 2)] for c in range(2)]
    formed = formed.reshape(groups * times // 2, 2, stations, samples)
    turned = lax.all_to_all(formed, ("stn", "tchunk"), 0, 0, axis_index_groups=classes, tiled=True)
    turned = turned.reshape(groups, times // 2, 2, stations, samples)
    row = lax.axis_index("tchunk").astype(jnp.int32).reshape(1)
    columns = groups * stations
    rows = columns // times
    scale = 1.0 / (samples * times)
    theirs = correlate_rows(row ^ 1, turned, rows, columns, scale, True, jnp.bfloat16, "correlate_theirs")
    swap = [(t, t ^ 1) for t in range(times)]
    arrived = [lax.ppermute(part, "tchunk", swap) for part in theirs]
    ours = correlate_rows(row, turned, rows, columns, scale, False, jnp.float32, "correlate_ours")
    result = add_parts(row, ours, arrived)
    return result[:, None, None]


def solution(mesh):
    in_specs = (P("stn", "chan", "tchunk", None), P("stn", "chan", None, None, None))
    out_specs = P(None, "chan", "stn", "tchunk", None)
    return jax.shard_map(local, mesh=mesh, in_specs=in_specs, out_specs=out_specs, check_vma=False)
```

```python
import jax
import jax.numpy as jnp
from jax import lax
from jax.experimental import pallas as pl
from jax.experimental.pallas import tpu as pltpu
from jax.sharding import PartitionSpec as P

NT_DIMS = (((1,), (1,)), ((), ()))
LAST = 2


def form_beams(copies, pieces, volt_hbm, wgt_hbm, out_ref, volt_ref, wgt_ref, held, sems):
    stations, beam_count = wgt_ref.shape[0], wgt_ref.shape[2]
    step = stations // pieces
    loads = []
    for p in range(pieces):
        part = pl.ds(p * step, step)
        loads.append(
            (
                pltpu.make_async_copy(wgt_hbm.at[part], wgt_ref.at[part], sems.at[0, p]),
                pltpu.make_async_copy(volt_hbm.at[part], volt_ref.at[part], sems.at[1, p]),
            )
        )
    for pair in loads:
        for load in pair:
            load.start()
    for s in range(0, stations, 2):
        if s % step == 0:
            for load in loads[s // step]:
                load.wait()
        matrices = []
        for q in (s, s + 1):
            w_re = wgt_ref[q, 0]
            w_im = wgt_ref[q, 1]
            matrices += [jnp.concatenate([w_re, -w_im], axis=-1), jnp.concatenate([w_im, w_re], axis=-1)]
        samples = volt_ref.shape[1]
        both = volt_ref[s : s + 2].reshape(2 * samples, volt_ref.shape[2])
        formed = lax.dot_general(jnp.concatenate(matrices, axis=0), both, NT_DIMS, preferred_element_type=jnp.float32)
        half = formed.shape[0] // 2
        held[s] = formed[:half, :samples].reshape(held.shape[1:])
        held[s + 1] = formed[half:, samples:].reshape(held.shape[1:])
    rounded = jnp.transpose(held[...], (2, 1, 0, 3)).astype(jnp.bfloat16)
    for b in range(beam_count):
        for c in range(copies):
            out_ref[b ^ 1, c] = rounded[b]


def correlate(scale, packed, row_ref, beams_ref, *out_refs):
    groups, times = beams_ref.shape[0], beams_ref.shape[1]
    row_count, columns = out_refs[0].shape[0], groups * beams_ref.shape[3]
    row_groups = row_count // beams_ref.shape[3]
    first = row_ref[0] * row_groups
    order = [lax.rem(first + (g ^ 1), groups) for g in range(groups)]
    total = None
    for t in range(times):
        re = [beams_ref[g, t, 0] for g in order]
        im = [beams_ref[g, t, 1] for g in order]
        left = jnp.concatenate([jnp.concatenate(re, axis=0), jnp.concatenate(im, axis=0)], axis=-1)
        row_re = jnp.concatenate(re[:row_groups], axis=0)
        row_im = jnp.concatenate(im[:row_groups], axis=0)
        left_rows = jnp.concatenate([row_re, row_im], axis=-1)
        other_rows = jnp.concatenate([row_im, -row_re], axis=-1)
        rows = jnp.concatenate([left_rows, other_rows], axis=0)
        part = lax.dot_general(rows, left, NT_DIMS, preferred_element_type=jnp.float32)
        total = part if total is None else total + part
    total = total * scale
    re, im = total[:row_count], total[row_count:]
    if packed:
        upper, _ = triangles(row_count)
        diagonal = jnp.where(upper, re[:, :row_count], im[:, :row_count])
        for (part, k), (to, at) in places(columns // row_count, row_count).items():
            block = (re, im)[part][:, k * row_count : (k + 1) * row_count]
            if k == 0:
                block = diagonal
            out_refs[to][:, at] = block.astype(out_refs[to].dtype)
    else:
        out_refs[0][...] = re.astype(out_refs[0].dtype)
        out_refs[1][...] = im.astype(out_refs[1].dtype)


def places(blocks, size):
    order = [(0, k) for k in range(blocks)] + [(1, k) for k in range(1, blocks)]
    first = len(order) - LAST
    return {b: (int(n >= first), slice((n % first) * size, (n % first + 1) * size)) for n, b in enumerate(order)}


def triangles(size):
    i = lax.broadcasted_iota(jnp.int32, (size, size), 0)
    j = lax.broadcasted_iota(jnp.int32, (size, size), 1)
    return i <= j, i > j


def correlate_rows(row, beams, rows, columns, scale, packed, dtype, name):
    widths = (2 * columns - (1 + LAST) * rows, LAST * rows) if packed else (columns, columns)
    return pl.pallas_call(
        lambda *refs: correlate(scale, packed, *refs),
        out_shape=[jax.ShapeDtypeStruct((rows, width), dtype) for width in widths],
        in_specs=[pl.BlockSpec(memory_space=pltpu.SMEM), pl.BlockSpec(memory_space=pltpu.VMEM)],
        out_specs=[pl.BlockSpec(memory_space=pltpu.VMEM)] * 2,
        compiler_params=pltpu.CompilerParams(vmem_limit_bytes=16 * 2**20),
        cost_estimate=pl.CostEstimate(flops=4 * rows * columns * 512, bytes_accessed=2**20, transcendentals=0),
        name=name,
    )(row, beams)


def add_rows(stage, row_ref, re_ref, im_ref, arrived_ref, *refs):
    out_hbm, total, sems = refs[-3:]
    rows, columns = re_ref.shape
    blocks = columns // rows
    here = [(b, at) for b, (to, at) in places(blocks, rows).items() if to == stage and b[1] > 0]
    if stage == 0:
        both = arrived_ref[:, :rows].astype(jnp.float32)
        upper, lower = triangles(rows)
        strict = jnp.where(lower, both, 0.0)
        here += [((0, 0), jnp.where(upper, both, both.T)), ((1, 0), strict - strict.T)]
    stores = []
    for n, ((part, k), block) in enumerate(here):
        if k > 0:
            block = arrived_ref[:, block].astype(jnp.float32)
        total[n] = (re_ref, im_ref)[part][:, k * rows : (k + 1) * rows] + block
        place = pl.multiple_of(lax.rem(row_ref[0] + k, blocks) * rows, rows)
        stores.append(pltpu.make_async_copy(total.at[n], out_hbm.at[part, :, pl.ds(place, rows)], sems.at[n]))
        stores[-1].start()
    for store in stores:
        store.wait()


def add_part(stage, row, ours, arrived, result):
    rows, columns = ours[0].shape
    vmem = pl.BlockSpec(memory_space=pltpu.VMEM)
    hbm = pl.BlockSpec(memory_space=pltpu.HBM)
    count = LAST if stage else 2 * (columns // rows) - LAST
    return pl.pallas_call(
        lambda *refs: add_rows(stage, *refs),
        out_shape=jax.ShapeDtypeStruct((2, rows, columns), jnp.float32),
        in_specs=[pl.BlockSpec(memory_space=pltpu.SMEM), vmem, vmem, vmem] + [hbm] * len(result),
        out_specs=hbm,
        scratch_shapes=[pltpu.VMEM((count, rows, rows), jnp.float32), pltpu.SemaphoreType.DMA((count,))],
        input_output_aliases={4: 0} if result else {},
        compiler_params=pltpu.CompilerParams(vmem_limit_bytes=16 * 2**20),
        cost_estimate=pl.CostEstimate(flops=rows * columns, bytes_accessed=8 * rows * columns, transcendentals=0),
        name="add_last" if stage else "add_first",
    )(row, *ours, arrived, *result)


def local(voltages, weights):
    stations, _, samples, width = voltages.shape
    beam_count = weights.shape[3]
    times = lax.axis_size("tchunk")
    groups = lax.axis_size("stn")
    vmem = pl.BlockSpec(memory_space=pltpu.VMEM)
    pieces = 2 if stations % 2 == 0 else 1
    formed = pl.pallas_call(
        lambda *refs: form_beams(times // 2, pieces, *refs),
        out_shape=jax.ShapeDtypeStruct((beam_count, times // 2, 2, stations, samples), jnp.bfloat16),
        in_specs=[pl.BlockSpec(memory_space=pltpu.HBM)] * 2,
        out_specs=vmem,
        scratch_shapes=[
            pltpu.VMEM((stations, samples, width), jnp.bfloat16),
            pltpu.VMEM((stations, 2, beam_count, width // 2), jnp.bfloat16),
            pltpu.VMEM((stations, 2, beam_count, samples), jnp.float32),
            pltpu.SemaphoreType.DMA((2, pieces)),
        ],
        compiler_params=pltpu.CompilerParams(vmem_limit_bytes=16 * 2**20),
        name="form_beams",
    )(
        pltpu.with_memory_space_constraint(voltages.reshape(stations, samples, width), pltpu.HBM),
        pltpu.with_memory_space_constraint(weights.reshape(stations, 2, beam_count, width // 2), pltpu.HBM),
    )
    classes = [[(g ^ 1) * times + t for g in range(groups) for t in range(c, times, 2)] for c in range(2)]
    formed = formed.reshape(groups * times // 2, 2, stations, samples)
    turned = lax.all_to_all(formed, ("stn", "tchunk"), 0, 0, axis_index_groups=classes, tiled=True)
    turned = turned.reshape(groups, times // 2, 2, stations, samples)
    row = lax.axis_index("tchunk").astype(jnp.int32).reshape(1)
    columns = groups * stations
    rows = columns // times
    scale = 1.0 / (samples * times)
    theirs = correlate_rows(row ^ 1, turned, rows, columns, scale, True, jnp.bfloat16, "correlate_theirs")
    swap = [(t, t ^ 1) for t in range(times)]
    arrived = [lax.ppermute(part, "tchunk", swap) for part in theirs]
    ours = correlate_rows(row, turned, rows, columns, scale, False, jnp.float32, "correlate_ours")
    result = add_part(0, row, ours, arrived[0], [])
    result = add_part(1, row, ours, arrived[1], [result])
    return result[:, None, None]


def solution(mesh):
    in_specs = (P("stn", "chan", "tchunk", None), P("stn", "chan", None, None, None))
    out_specs = P(None, "chan", "stn", "tchunk", None)
    return jax.shard_map(local, mesh=mesh, in_specs=in_specs, out_specs=out_specs, check_vma=False)
```
